512 devices in a mesh: pipe: 16 (over y_lo, x, core), tensor: 32 (over z, y_hi).
Axes of the slice: x: 4, y: 4 (y_hi: 2, y_lo: 2; y = y_hi * 2 + y_lo), z: 16, core: 2. Of those that a mesh axis runs over, the one named last changes fastest.
Arguments:
- w_up: bfloat16 [29696, 14848], P('tensor', 'pipe'), may hold values from -0.046875 to 0.046875
- inputs_a: bfloat16 [512, 14848], P('tensor', 'pipe'), may hold values from -6 to 6
- grad_a: bfloat16 [512, 29696], P(None, 'tensor'), may hold values from -0.29882812 to 0.29882812
- grad_b: bfloat16 [256, 29696], P(None, 'tensor'), may hold values from -6 to 6
Outputs:
- weight_grad: bfloat16 [29696, 14848], P('tensor', 'pipe')
- input_grad: bfloat16 [256, 14848], P('tensor', 'pipe')
The draws below stay inside these ranges and needn't reach their ends.
All inputs are finite; a program needn't handle non-finite values.
Results may differ from the reference program's by a relative error of at most 0.0049.
Values may be sent and summed in bfloat16 or wider, within the bound.
A program may use at most 64 MiB of HBM per device.

```python
import jax
import jax.numpy as jnp
from jax import lax

D = 14848
HID_DEV = 928
HIDDEN_SIZE = 29696
SEQ_A = 512
SEQ_B = 256
N_TENSOR = 32


def strengthened(values, own_key, source, target, parts, factor):
    def block_of(dim):
        return (jnp.arange(values.shape[dim]) // (values.shape[dim] // parts)).reshape((-1,) + (1,) * (values.ndim - 1 - dim))

    first = jax.random.permutation(own_key, parts)[block_of(target)]
    other_side = (block_of(target) + parts // 2) % parts
    return jnp.where((block_of(source) == first) | (block_of(source) == other_side), factor * values, values)


def levels(stream_key, shape, split, low, high):
    def one(position, parts):
        heights = jax.random.uniform(jax.random.fold_in(jax.random.fold_in(stream_key, 6), position), (parts,), jnp.float32, low / len(split), high / len(split))
        return jnp.repeat(jnp.exp(heights), shape[position] // parts).reshape((-1,) + (1,) * (len(shape) - position - 1))

    level = one(*split[0])
    for cut in split[1:]:
        level = level * one(*cut)
    return level


def scatter_about(rng, shape, scale, most, pieces=(), dtype=jnp.bfloat16):
    level = levels(rng, shape, pieces, -0.22, 0.18) if pieces else 1.0
    entries = jax.random.normal(rng, shape, jnp.float32) * scale * level
    return jnp.minimum(jnp.maximum(entries, -most), most).astype(dtype)


def bell_draw_with(key, shape, scale, bound, shards, heavy, dtype=jnp.bfloat16):
    result = scale * jax.random.normal(key, shape, jnp.float32)
    if shards:
        result = result * levels(key, shape, shards, -0.22, 0.18)
    return jnp.clip(strengthened(result, jax.random.fold_in(key, 3), *heavy), -bound, bound).astype(dtype)


def setup_inputs(seed: int = 0) -> dict:
    splits = jax.random.split(jax.random.key(seed), 5)
    return {
        "w_up": scatter_about(splits[0], (HIDDEN_SIZE, D), D ** -0.5, 0.046875, ((0, 32), (1, 16))),
        "inputs_a": scatter_about(splits[1], (SEQ_A, D), 1.0, 6.0, ((0, 32), (1, 16))),
        "grad_a": scatter_about(splits[2], (SEQ_A, HIDDEN_SIZE), 0.05, 0.29882812, ((1, 32),)),
        "grad_b": bell_draw_with(splits[3], (SEQ_B, HIDDEN_SIZE), 1.0, 6.0, ((1, 32),), (1, 0, 32, 2.75)),
    }


def slope(pre):
    cdf = 0.5 * (1.0 + jax.scipy.special.erf(pre * 0.7071067811865476))
    pdf = jnp.exp(-0.5 * pre * pre) * 0.3989422804014327
    return cdf + pre * pdf


def reference(w_up, inputs_a, grad_a, grad_b):
    pre = lax.dot_general(inputs_a, w_up, (((1,), (1,)), ((), ())), preferred_element_type=jnp.float32)
    delta = (grad_a.astype(jnp.float32) * slope(pre)).astype(jnp.bfloat16)
    delta_blocks = jnp.transpose(delta.reshape(delta.shape[0], N_TENSOR, HID_DEV), (1, 0, 2))

    def grad_block(block):
        return lax.dot_general(block, inputs_a, (((0,), (0,)), ((), ())), preferred_element_type=jnp.float32).astype(jnp.bfloat16)

    weight_grad = lax.map(grad_block, delta_blocks).reshape(w_up.shape)
    input_grad = jnp.dot(grad_b, w_up, preferred_element_type=jnp.float32).astype(jnp.bfloat16)
    return weight_grad, input_grad
```

```python
import functools

import jax
import jax.numpy as jnp
from jax import lax
from jax.experimental import pallas as pl
from jax.experimental.pallas import tpu as pltpu
from jax.sharding import PartitionSpec as P

MESH = pl.DeviceIdType.MESH
F32 = jnp.float32
BF16 = jnp.bfloat16


def slope(pre):
    cdf = 0.5 * (1.0 + lax.erf(pre * 0.7071067811865476))
    pdf = jnp.exp(-0.5 * pre * pre) * 0.3989422804014327
    return cdf + pre * pdf


class Layout:
    def __init__(self, nz, nx, nyl):
        self.nz, self.nx, self.nyl = nz, nx, nyl
        self.reach = nz // 4
        self.chips = nx * nyl

    def slot(self, dz, yr):
        h, nz = self.reach, self.nz
        dz = (dz + h) % nz - h
        first = dz <= (h if yr == 0 else h - 1) and dz >= (-h if yr == 0 else 1 - h)
        if first:
            return dz + h if yr == 0 else dz + 3 * h
        dz = dz % nz
        return nz + (dz - h - 1 if yr == 0 else dz + h - 1)

    def block_of(self, half, j):
        h, nz = self.reach, self.nz
        if half == 0:
            yr = j // (2 * h + 1)
            return j - h - yr * 2 * h, yr
        yr = (j + nz - (2 * h - 1)) // nz
        return j + h + 1 - 2 * h * yr, yr


def kernel(lay, rows, w_hbm, a_hbm, ga_hbm, gb_hbm, wg_hbm, ig_ref,
           w, g, ga, gb, q, ysend, yrecv, tot, zsend, zrecv,
           p, csend, crecv, own, rsend, rrecv, d, acc, out,
           load_sem, ag_send, ag_recv, y_send, y_recv, z_send, z_recv,
           c_send, c_recv, r_send, r_recv, d_send, d_recv, f_send, f_recv, out_sem):
    nz, nx, nyl = lay.nz, lay.nx, lay.nyl
    tensor, pipe = lax.axis_index("tensor"), lax.axis_index("pipe")
    z, yh = tensor // 2, tensor % 2
    core, chip = pipe % 2, pipe // 2
    yl, x = chip // nx, chip % nx
    half_rows = nz * rows
    core_rows = half_rows // 2

    def at_tensor(dz, dy):
        return {"tensor": ((z + dz + nz) % nz) * 2 + (yh + dy) % 2}

    def at_chip(dyl, dx):
        return {"pipe": (((yl + dyl) % nyl) * nx + (x + dx) % nx) * 2 + core}

    other_core = {"pipe": chip * 2 + (1 - core)}
    others = [(a, b) for a in range(nyl) for b in range(nx) if a or b]

    def remote(src, dst, send, recv, to):
        return pltpu.make_async_remote_copy(
            src_ref=src, dst_ref=dst, send_sem=send, recv_sem=recv, device_id=to, device_id_type=MESH)

    sent = []

    def block(ref, slot):
        return ref.at[pl.ds(slot * rows, rows)]

    load_a = pltpu.make_async_copy(a_hbm, block(g, lay.slot(0, 0)), load_sem.at[0])
    load_w = pltpu.make_async_copy(w_hbm, w, load_sem.at[1])
    load_gb = pltpu.make_async_copy(gb_hbm, gb, load_sem.at[2])
    load_a.start()
    load_w.start()
    load_gb.start()
    load_ga = []
    for half in range(2):
        dz, yr = lay.block_of(half, core * lay.chips + chip)
        t = ((z + dz + nz) % nz) * 2 + (yh + yr) % 2
        c = pltpu.make_async_copy(ga_hbm.at[pl.ds(pl.multiple_of(t * rows, rows), rows)], ga.at[half], load_sem.at[3 + half])
        c.start()
        load_ga.append(c)

    barrier = pltpu.get_barrier_semaphore()
    greet = [at_tensor(dz, 0) for dz in range(1, nz)] + [at_tensor(0, 1), other_core]
    greet += [at_chip(*o) for o in others]
    for to in greet:
        pl.semaphore_signal(barrier, inc=1, device_id=to, device_id_type=MESH)
    pl.semaphore_wait(barrier, len(greet))

    def gather_copy(src, dz, yr, to_left):
        s = lay.slot(dz, yr)
        return remote(src, block(g, s), ag_send.at[s], ag_recv.at[s], at_tensor(-1 if to_left else 1, 0))

    def forward(dz, yr):
        src = block(g, lay.slot(dz, yr))
        last = nz // 2
        for to_left in (True, False):
            if to_left and not (dz >= 0):
                continue
            if not to_left and not (dz <= 0):
                continue
            step = abs(dz) + 1
            if step > last or (step == last and (yr == 0) != to_left):
                continue
            c = gather_copy(a_hbm if (dz == 0 and yr == 0) else src, step if to_left else -step, yr, to_left)
            c.start()
            sent.append(c)

    def arrive(dz, yr):
        s = lay.slot(dz, yr)
        remote(block(g, s), block(g, s), ag_send.at[s], ag_recv.at[s], at_tensor(1, 0)).wait_recv()
        forward(dz, yr)

    s01 = lay.slot(0, 1)
    forward(0, 0)
    c = remote(a_hbm, block(g, s01), ag_send.at[s01], ag_recv.at[s01], at_tensor(0, 1))
    c.start()
    sent.append(c)

    load_gb.wait()
    load_w.wait()
    width = w.shape[1]
    q[...] = jnp.dot(gb[...], w[...], preferred_element_type=F32).reshape(q.shape)
    ysend[...] = q[:, pl.ds(1 - yh, 1)].reshape(nz * q.shape[2], width).astype(BF16)
    yc = remote(ysend, yrecv, y_send, y_recv, at_tensor(0, 1))
    yc.start()
    load_a.wait()

    def sum_b():
        yc.wait_recv()
        tot[:, 0:width] = q[:, pl.ds(yh, 1)].reshape(nz * q.shape[2], width) + yrecv[...].astype(F32)
        wide = 2 * zsend.shape[2]
        if wide > width:
            tot[:, width:wide] = jnp.zeros((tot.shape[0], wide - width), F32)
        left = tot[:, 0:wide // 2].reshape(nz, q.shape[2], wide // 2)
        right = tot[:, wide // 2:wide].reshape(nz, q.shape[2], wide // 2)
        zsend[...] = jnp.concatenate([left, right], axis=1).astype(BF16)

    zcs = []

    def send_b():
        for dz in [s * k for k in range(1, nz // 2 + 1) for s in (1, -1)][:nz - 1]:
            c = remote(zsend.at[(z + dz + nz) % nz], zrecv.at[dz % nz], z_send.at[dz % nz], z_recv.at[dz % nz], at_tensor(dz, 0))
            c.start()
            zcs.append(c)

    def finish_b():
        depth = q.shape[2]
        wide = zsend.shape[2]
        mine = tot[pl.ds(pl.multiple_of(z * depth, depth), depth), :]
        total = jnp.concatenate([mine[:, 0:wide], mine[:, wide:2 * wide]], axis=0)
        for c in zcs:
            c.wait_recv()
        for dz in range(1, nz):
            total += zrecv[dz].astype(F32)
        ig_ref[:, 0:wide] = total[0:depth].astype(BF16)
        ig_ref[:, wide:width] = total[depth:2 * depth, 0:width - wide].astype(BF16)

    core_copies, chip_copies, delta_copies, core_forwards = [None, None], [[], []], [[], []], [[], []]

    def project(half):
        p[half] = lax.dot_general(
            g[pl.ds(half * half_rows, half_rows), :], w[...], (((1,), (1,)), ((), ())), preferred_element_type=F32)
        csend[half] = p[half, pl.ds(pl.multiple_of((1 - core) * core_rows, core_rows), core_rows), :].astype(BF16)
        c = remote(csend.at[half], crecv.at[half], c_send.at[half], c_recv.at[half], other_core)
        c.start()
        core_copies[half] = c

    def reduce_send(half):
        core_copies[half].wait_recv()
        own[half] = p[half, pl.ds(pl.multiple_of(core * core_rows, core_rows), core_rows), :] + crecv[half].astype(F32)
        rsend[half] = own[half].astype(BF16)
        for k, (dyl, dx) in enumerate(others):
            to = ((yl + dyl) % nyl) * nx + (x + dx) % nx
            c = remote(rsend.at[half, pl.ds(pl.multiple_of(to * rows, rows), rows)], rrecv.at[half, k],
                       r_send.at[half, k], r_recv.at[half, k], at_chip(dyl, dx))
            c.start()
            chip_copies[half].append(c)

    def d_block(half, which_core, which_chip):
        start = ((half * 2 + which_core) * lay.chips + which_chip) * rows
        return d.at[pl.ds(pl.multiple_of(start, rows), rows)]

    def activate(half):
        for c in chip_copies[half]:
            c.wait_recv()
        pre = own[half, pl.ds(pl.multiple_of(chip * rows, rows), rows), :]
        for k in range(len(others)):
            pre += rrecv[half, k].astype(F32)
        load_ga[half].wait()
        mine = d_block(half, core, chip)
        mine[...] = (ga[half].astype(F32) * slope(pre)).astype(BF16)
        for k, (dyl, dx) in enumerate(others):
            c = remote(mine, mine, d_send.at[half, k], d_recv.at[half, k], at_chip(dyl, dx))
            c.start()
            delta_copies[half].append(c)
        n = len(others)
        c = remote(mine, mine, f_send.at[half, n], f_recv.at[half, n], other_core)
        c.start()
        core_forwards[half].append(c)

    def spread(half):
        for k, (dyl, dx) in enumerate(others):
            source = ((yl - dyl + nyl) % nyl) * nx + (x - dx + nx) % nx
            b = d_block(half, core, source)
            remote(b, b, d_send.at[half, k], d_recv.at[half, k], at_chip(dyl, dx)).wait_recv()
            c = remote(b, b, f_send.at[half, k], f_recv.at[half, k], other_core)
            c.start()
            core_forwards[half].append(c)

    def collect(half):
        for k, (dyl, dx) in enumerate(others):
            source = ((yl - dyl + nyl) % nyl) * nx + (x - dx + nx) % nx
            b = d_block(half, 1 - core, source)
            remote(b, b, f_send.at[half, k], f_recv.at[half, k], other_core).wait_recv()
        n = len(others)
        b = d_block(half, 1 - core, chip)
        remote(b, b, f_send.at[half, n], f_recv.at[half, n], other_core).wait_recv()

    def weight(half, lo, hi):
        return lax.dot_general(
            d[pl.ds(half * half_rows, half_rows), lo:hi], g[pl.ds(half * half_rows, half_rows), :],
            (((0,), (0,)), ((), ())), preferred_element_type=F32)

    last = nz // 2
    h = lay.reach
    arrive_later = []
    arrive(0, 1)
    for s in range(1, h):
        for yr in (0, 1):
            arrive(s, yr)
            arrive(-s, yr)
    arrive(h, 0)
    arrive(-h, 0)
    project(0)
    if h < last:
        arrive(h, 1)
        arrive(-h, 1)
    reduce_send(0)
    rest = [(s * sign, yr) for s in range(h + 1, last) for yr in (0, 1) for sign in (1, -1)]
    cut = (len(rest) * 2) // 3
    for b in rest[:cut]:
        arrive(*b)
    sum_b()
    activate(0)
    for b in rest[cut:]:
        arrive(*b)
    arrive(last, 0)
    arrive(last, 1)
    project(1)
    spread(0)
    send_b()
    reduce_send(1)
    collect(0)
    hid = w.shape[0]
    cuts = list(range(0, hid, 256)) + [hid]
    for lo, hi in zip(cuts[:-1], cuts[1:]):
        acc[lo:hi, :] = weight(0, lo, hi)
    activate(1)
    spread(1)
    finish_b()
    collect(1)
    outs = []
    for i, (lo, hi) in enumerate(zip(cuts[:-1], cuts[1:])):
        out[lo:hi, :] = (acc[lo:hi, :] + weight(1, lo, hi)).astype(BF16)
        c = pltpu.make_async_copy(out.at[pl.ds(lo, hi - lo)], wg_hbm.at[pl.ds(lo, hi - lo)], out_sem.at[i])
        c.start()
        outs.append(c)
    for c in sent + [yc] + zcs + core_copies + chip_copies[0] + chip_copies[1] + delta_copies[0] + delta_copies[1]:
        c.wait_send()
    for c in core_forwards[0] + core_forwards[1]:
        c.wait_send()
    for c in outs:
        c.wait()


def build(mesh, lay):
    def step(w_up, inputs_a, grad_a, grad_b):
        hid, width = w_up.shape
        rows = inputs_a.shape[0]
        nz = lay.nz
        seq_b = grad_b.shape[0]
        depth = seq_b // (2 * nz)
        half_rows = nz * rows
        n = lay.chips - 1
        wide = -(-width // 256) * 128
        dma = pltpu.SemaphoreType.DMA
        flops = 2 * hid * width * (4 * half_rows + seq_b)
        return pl.pallas_call(
            functools.partial(kernel, lay, rows),
            out_shape=(jax.ShapeDtypeStruct((hid, width), BF16), jax.ShapeDtypeStruct((depth, width), BF16)),
            in_specs=[pl.BlockSpec(memory_space=pl.ANY)] * 4,
            out_specs=(pl.BlockSpec(memory_space=pl.ANY), pl.BlockSpec(memory_space=pltpu.VMEM)),
            scratch_shapes=[
                pltpu.VMEM((hid, width), BF16),
                pltpu.VMEM((2 * half_rows, width), BF16),
                pltpu.VMEM((2, rows, hid), BF16),
                pltpu.VMEM((seq_b, hid), BF16),
                pltpu.VMEM((nz, 2, depth, width), F32),
                pltpu.VMEM((nz * depth, width), BF16),
                pltpu.VMEM((nz * depth, width), BF16),
                pltpu.VMEM((nz * depth, 2 * wide), F32),
                pltpu.VMEM((nz, 2 * depth, wide), BF16),
                pltpu.VMEM((nz, 2 * depth, wide), BF16),
                pltpu.VMEM((2, half_rows, hid), F32),
                pltpu.VMEM((2, half_rows // 2, hid), BF16),
                pltpu.VMEM((2, half_rows // 2, hid), BF16),
                pltpu.VMEM((2, half_rows // 2, hid), F32),
                pltpu.VMEM((2, half_rows // 2, hid), BF16),
                pltpu.VMEM((2, n, rows, hid), BF16),
                pltpu.VMEM((2 * half_rows, hid), BF16),
                pltpu.VMEM((hid, width), F32),
                pltpu.VMEM((hid, width), BF16),
                dma((5,)), dma((2 * nz,)), dma((2 * nz,)), dma, dma, dma((nz,)), dma((nz,)),
                dma((2,)), dma((2,)), dma((2, n)), dma((2, n)), dma((2, n)), dma((2, n)), dma((2, n + 1)), dma((2, n + 1)), dma((8,)),
            ],
            compiler_params=pltpu.CompilerParams(
                collective_id=0, has_side_effects=True, vmem_limit_bytes=40 * 1024 * 1024),
            cost_estimate=pl.CostEstimate(flops=flops, bytes_accessed=5_000_000, transcendentals=100_000),
        )(w_up, inputs_a, grad_a, grad_b)

    return jax.shard_map(
        step,
        mesh=mesh,
        in_specs=(P("tensor", "pipe"), P("tensor", "pipe"), P(None, "tensor"), P(None, "tensor")),
        out_specs=(P("tensor", "pipe"), P("tensor", "pipe")),
        check_vma=False,
    )


def solution(mesh):
    nz = mesh.shape["tensor"] // 2
    nyl = 2
    return build(mesh, Layout(nz, mesh.shape["pipe"] // (2 * nyl), nyl))
```

```python
import functools

import jax
import jax.numpy as jnp
from jax import lax
from jax.experimental import pallas as pl
from jax.experimental.pallas import tpu as pltpu
from jax.sharding import PartitionSpec as P

MESH = pl.DeviceIdType.MESH
F32 = jnp.float32
BF16 = jnp.bfloat16


def slope(pre):
    cdf = 0.5 * (1.0 + lax.erf(pre * 0.7071067811865476))
    pdf = jnp.exp(-0.5 * pre * pre) * 0.3989422804014327
    return cdf + pre * pdf


class Layout:
    def __init__(self, nz, nx, nyl):
        self.nz, self.nx, self.nyl = nz, nx, nyl
        self.chips = nx * nyl
        last = nz // 2
        self.direct = (6, 3, 1) if nz == 16 else (1,)
        self.relays = {1: (2,), 3: (4,), 6: (8, 7, 5)} if nz == 16 else {1: (2,)}
        distances = (1, 3, 6, 2, 4, 5, 7) if nz == 16 else (1,)
        arrivals = [0] + [d * s for d in distances for s in (1, -1)] + [nz // 2]
        order = [(d, yr) for yr in (0, 1) for d in arrivals]
        self.order = order

    def slot(self, dz, yr):
        dz = dz % self.nz
        return self.order.index((dz if dz <= self.nz // 2 else dz - self.nz, yr))


def kernel(lay, rows, w_hbm, a_hbm, ga_hbm, gb_hbm, wg_hbm, ig_ref,
           w, g, ga, gat, gb, q, ysend, yrecv, tot, zsend, zrecv,
           p, csend, crecv, own, rsend, rrecv, d, acc, out,
           load_sem, ag_send, ag_recv, y_send, y_recv, z_send, z_recv,
           c_send, c_recv, r_send, r_recv, d_send, d_recv, f_send, f_recv, out_sem):
    nz, nx, nyl = lay.nz, lay.nx, lay.nyl
    tensor, pipe = lax.axis_index("tensor"), lax.axis_index("pipe")
    z, yh = tensor // 2, tensor % 2
    core, chip = pipe % 2, pipe // 2
    yl, x = chip // nx, chip % nx
    half_rows = nz * rows
    core_rows = half_rows // 2

    def at_tensor(dz, dy):
        return {"tensor": ((z + dz + nz) % nz) * 2 + (yh + dy) % 2}

    def at_chip(dyl, dx):
        return {"pipe": (((yl + dyl) % nyl) * nx + (x + dx) % nx) * 2 + core}

    other_core = {"pipe": chip * 2 + (1 - core)}
    others = [(a, b) for a in range(nyl) for b in range(nx) if a or b]

    def remote(src, dst, send, recv, to):
        return pltpu.make_async_remote_copy(
            src_ref=src, dst_ref=dst, send_sem=send, recv_sem=recv, device_id=to, device_id_type=MESH)

    sent = []

    def block(slot):
        return g.at[pl.ds(slot * rows, rows)]

    load_a = pltpu.make_async_copy(a_hbm, block(lay.slot(0, 0)), load_sem.at[0])
    load_w = pltpu.make_async_copy(w_hbm, w, load_sem.at[1])
    load_gb = pltpu.make_async_copy(gb_hbm, gb, load_sem.at[2])
    load_a.start()
    load_w.start()
    load_gb.start()
    load_ga, ga_row = [], []
    lanes = ga.shape[2]
    for half in range(2):
        dz, yr = 0, 0
        for j in range(nz):
            hit = 1 - jnp.minimum(jnp.abs(core * lay.chips + chip - j), 1)
            block_z, block_y = lay.order[half * nz + j]
            dz, yr = dz + hit * (block_z % nz), yr + hit * block_y
        t = ((z + dz) % nz) * 2 + (yh + yr) % 2
        start = pl.multiple_of((t * rows // lanes) * lanes, lanes)
        c = pltpu.make_async_copy(ga_hbm.at[:, pl.ds(start, lanes)], ga.at[half], load_sem.at[3 + half])
        c.start()
        load_ga.append(c)
        ga_row.append(pl.multiple_of(t * rows % lanes, rows))

    barrier = pltpu.get_barrier_semaphore()
    greet = [at_tensor(dz, 0) for dz in range(1, nz)] + [at_tensor(0, 1), other_core]
    greet += [at_chip(*o) for o in others]
    for to in greet:
        pl.semaphore_signal(barrier, inc=1, device_id=to, device_id_type=MESH)
    pl.semaphore_wait(barrier, len(greet))

    def gather(src, dz, yr, to):
        s = lay.slot(dz, yr)
        return remote(src, block(s), ag_send.at[s], ag_recv.at[s], to)

    def start_gather():
        copies = [gather(a_hbm, d * s, 0, at_tensor(-d * s, 0)) for d in lay.direct for s in (1, -1)]
        copies.insert(2, gather(a_hbm, 0, 1, at_tensor(0, 1)))
        for c in copies:
            c.start()
        sent.extend(copies)

    def arrive(dz, yr):
        src = block(lay.slot(dz, yr))
        gather(src, dz, yr, at_tensor(1, 0)).wait_recv()
        if yr == 0:
            sign = 1 if dz > 0 else -1
            copies = []
            for d in lay.relays.get(abs(dz), ()):
                if d < nz // 2 or dz > 0:
                    copies.append(gather(src, d * sign, 0, at_tensor(dz - d * sign, 0)))
            copies.append(gather(src, dz, 1, at_tensor(0, 1)))
            for c in copies:
                c.start()
            sent.extend(copies)

    width = w.shape[1]
    yc = remote(ysend, yrecv, y_send, y_recv, at_tensor(0, 1))

    def local_b():
        load_gb.wait()
        load_w.wait()
        q[...] = lax.dot_general(gb[...], w[...], (((0,), (0,)), ((), ())), preferred_element_type=F32).reshape(q.shape)
        ysend[...] = q[:, pl.ds(1 - yh, 1)].reshape(nz * q.shape[2], width).astype(BF16)

    def exchange_b():
        yc.start()
        sent.append(yc)

    def turn_ga():
        for half in range(2):
            load_ga[half].wait()
            gat[half] = ga[half].T

    def sum_b():
        yc.wait_recv()
        tot[:, 0:width] = q[:, pl.ds(yh, 1)].reshape(nz * q.shape[2], width) + yrecv[...].astype(F32)
        wide = 2 * zsend.shape[2]
        if wide > width:
            tot[:, width:wide] = jnp.zeros((tot.shape[0], wide - width), F32)
        left = tot[:, 0:wide // 2].reshape(nz, q.shape[2], wide // 2)
        right = tot[:, wide // 2:wide].reshape(nz, q.shape[2], wide // 2)
        zsend[...] = jnp.concatenate([left, right], axis=1).astype(BF16)

    zcs = []

    def send_b():
        for dz in [s * k for k in range(1, nz // 2 + 1) for s in (1, -1)][:nz - 1]:
            c = remote(zsend.at[(z + dz + nz) % nz], zrecv.at[dz % nz], z_send.at[dz % nz], z_recv.at[dz % nz], at_tensor(dz, 0))
            c.start()
            zcs.append(c)

    def finish_b():
        depth = q.shape[2]
        wide = zsend.shape[2]
        mine = tot[pl.ds(pl.multiple_of(z * depth, depth), depth), :]
        total = jnp.concatenate([mine[:, 0:wide], mine[:, wide:2 * wide]], axis=0)
        for c in zcs:
            c.wait_recv()
        for dz in range(1, nz):
            total += zrecv[dz].astype(F32)
        ig_ref[:, 0:wide] = total[0:depth].astype(BF16)
        ig_ref[:, wide:width] = total[depth:2 * depth, 0:width - wide].astype(BF16)

    core_copies, chip_copies, delta_copies, core_forwards = [None, None], [[], []], [[], []], [[], []]

    def project(half):
        p[half] = lax.dot_general(
            g[pl.ds(half * half_rows, half_rows), :], w[...], (((1,), (1,)), ((), ())), preferred_element_type=F32)
        csend[half] = p[half, pl.ds(pl.multiple_of((1 - core) * core_rows, core_rows), core_rows), :].astype(BF16)
        c = remote(csend.at[half], crecv.at[half], c_send.at[half], c_recv.at[half], other_core)
        c.start()
        core_copies[half] = c

    def reduce_send(half):
        core_copies[half].wait_recv()
        own[half] = p[half, pl.ds(pl.multiple_of(core * core_rows, core_rows), core_rows), :] + crecv[half].astype(F32)
        rsend[half] = own[half].astype(BF16)
        for k, (dyl, dx) in enumerate(others):
            to = ((yl + dyl) % nyl) * nx + (x + dx) % nx
            c = remote(rsend.at[half, pl.ds(pl.multiple_of(to * rows, rows), rows)], rrecv.at[half, k],
                       r_send.at[half, k], r_recv.at[half, k], at_chip(dyl, dx))
            c.start()
            chip_copies[half].append(c)

    def d_block(half, which_core, which_chip):
        start = ((half * 2 + which_core) * lay.chips + which_chip) * rows
        return d.at[pl.ds(pl.multiple_of(start, rows), rows)]

    def activate(half):
        for c in chip_copies[half]:
            c.wait_recv()
        pre = own[half, pl.ds(pl.multiple_of(chip * rows, rows), rows), :]
        for k in range(len(others)):
            pre += rrecv[half, k].astype(F32)
        mine = d_block(half, core, chip)
        mine[...] = (gat[half, pl.ds(ga_row[half], rows), :].astype(F32) * slope(pre)).astype(BF16)
        for k, (dyl, dx) in enumerate(others):
            c = remote(mine, mine, d_send.at[half, k], d_recv.at[half, k], at_chip(dyl, dx))
            c.start()
            delta_copies[half].append(c)
        n = len(others)
        c = remote(mine, mine, f_send.at[half, n], f_recv.at[half, n], other_core)
        c.start()
        core_forwards[half].append(c)

    def spread(half):
        for k, (dyl, dx) in enumerate(others):
            source = ((yl - dyl + nyl) % nyl) * nx + (x - dx + nx) % nx
            b = d_block(half, core, source)
            remote(b, b, d_send.at[half, k], d_recv.at[half, k], at_chip(dyl, dx)).wait_recv()
            c = remote(b, b, f_send.at[half, k], f_recv.at[half, k], other_core)
            c.start()
            core_forwards[half].append(c)

    def collect(half):
        for k, (dyl, dx) in enumerate(others):
            source = ((yl - dyl + nyl) % nyl) * nx + (x - dx + nx) % nx
            b = d_block(half, 1 - core, source)
            remote(b, b, f_send.at[half, k], f_recv.at[half, k], other_core).wait_recv()
        n = len(others)
        b = d_block(half, 1 - core, chip)
        remote(b, b, f_send.at[half, n], f_recv.at[half, n], other_core).wait_recv()

    def weight(half, lo, hi):
        return lax.dot_general(
            d[pl.ds(half * half_rows, half_rows), lo:hi], g[pl.ds(half * half_rows, half_rows), :],
            (((0,), (0,)), ((), ())), preferred_element_type=F32)

    hid = w.shape[0]
    cuts = list(range(0, hid, 256)) + [hid]
    outs = []

    def weigh(half):
        if half == 0:
            for lo, hi in zip(cuts[:-1], cuts[1:]):
                acc[lo:hi, :] = weight(0, lo, hi)
            return
        for i, (lo, hi) in enumerate(zip(cuts[:-1], cuts[1:])):
            out[lo:hi, :] = (acc[lo:hi, :] + weight(1, lo, hi)).astype(BF16)
            c = pltpu.make_async_copy(out.at[pl.ds(lo, hi - lo)], wg_hbm.at[pl.ds(lo, hi - lo)], out_sem.at[i])
            c.start()
            outs.append(c)

    start_gather()
    local_b()
    exchange_b()
    for b in lay.order[1:nz]:
        arrive(*b)
    load_a.wait()
    project(0)
    turn_ga()
    reduce_send(0)
    for b in lay.order[nz:]:
        arrive(*b)
    project(1)
    sum_b()
    send_b()
    reduce_send(1)
    activate(0)
    activate(1)
    spread(0)
    finish_b()
    collect(0)
    weigh(0)
    spread(1)
    collect(1)
    weigh(1)
    for c in sent + zcs + core_copies + chip_copies[0] + chip_copies[1] + delta_copies[0] + delta_copies[1]:
        c.wait_send()
    for c in core_forwards[0] + core_forwards[1]:
        c.wait_send()
    for c in outs:
        c.wait()


def build(mesh, lay):
    def step(w_up, inputs_a, grad_a, grad_b):
        hid, width = w_up.shape
        rows = inputs_a.shape[0]
        nz = lay.nz
        seq_b = grad_b.shape[0]
        depth = seq_b // (2 * nz)
        half_rows = nz * rows
        n = lay.chips - 1
        wide = -(-width // 256) * 128
        dma = pltpu.SemaphoreType.DMA
        flops = 2 * hid * width * (4 * half_rows + seq_b)
        return pl.pallas_call(
            functools.partial(kernel, lay, rows),
            out_shape=(jax.ShapeDtypeStruct((hid, width), BF16), jax.ShapeDtypeStruct((depth, width), BF16)),
            in_specs=[pl.BlockSpec(memory_space=pl.ANY)] * 4,
            out_specs=(pl.BlockSpec(memory_space=pl.ANY), pl.BlockSpec(memory_space=pltpu.VMEM)),
            scratch_shapes=[
                pltpu.VMEM((hid, width), BF16),
                pltpu.VMEM((2 * half_rows, width), BF16),
                pltpu.VMEM((2, hid, 128), BF16),
                pltpu.VMEM((2, 128, hid), BF16),
                pltpu.VMEM((hid, seq_b), BF16),
                pltpu.VMEM((nz, 2, depth, width), F32),
                pltpu.VMEM((nz * depth, width), BF16),
                pltpu.VMEM((nz * depth, width), BF16),
                pltpu.VMEM((nz * depth, 2 * wide), F32),
                pltpu.VMEM((nz, 2 * depth, wide), BF16),
                pltpu.VMEM((nz, 2 * depth, wide), BF16),
                pltpu.VMEM((2, half_rows, hid), F32),
                pltpu.VMEM((2, half_rows // 2, hid), BF16),
                pltpu.VMEM((2, half_rows // 2, hid), BF16),
                pltpu.VMEM((2, half_rows // 2, hid), F32),
                pltpu.VMEM((2, half_rows // 2, hid), BF16),
                pltpu.VMEM((2, n, rows, hid), BF16),
                pltpu.VMEM((2 * half_rows, hid), BF16),
                pltpu.VMEM((hid, width), F32),
                pltpu.VMEM((hid, width), BF16),
                dma((5,)), dma((2 * nz,)), dma((2 * nz,)), dma, dma, dma((nz,)), dma((nz,)),
                dma((2,)), dma((2,)), dma((2, n)), dma((2, n)), dma((2, n)), dma((2, n)), dma((2, n + 1)), dma((2, n + 1)), dma((8,)),
            ],
            compiler_params=pltpu.CompilerParams(
                collective_id=0, has_side_effects=True, vmem_limit_bytes=62 * 1024 * 1024),
            cost_estimate=pl.CostEstimate(flops=flops, bytes_accessed=5_000_000, transcendentals=100_000),
        )(w_up, inputs_a, grad_a.T, grad_b.T)

    return jax.shard_map(
        step,
        mesh=mesh,
        in_specs=(P("tensor", "pipe"), P("tensor", "pipe"), P(None, "tensor"), P(None, "tensor")),
        out_specs=(P("tensor", "pipe"), P("tensor", "pipe")),
        check_vma=False,
    )


def solution(mesh):
    nz = mesh.shape["tensor"] // 2
    nyl = 2
    return build(mesh, Layout(nz, mesh.shape["pipe"] // (2 * nyl), nyl))
```

```python
import functools

import jax
import jax.numpy as jnp
from jax import lax
from jax.experimental import pallas as pl
from jax.experimental.pallas import tpu as pltpu
from jax.sharding import PartitionSpec as P

MESH = pl.DeviceIdType.MESH
F32 = jnp.float32
BF16 = jnp.bfloat16


def slope(pre):
    cdf = 0.5 * (1.0 + lax.erf(pre * 0.7071067811865476))
    pdf = jnp.exp(-0.5 * pre * pre) * 0.3989422804014327
    return cdf + pre * pdf


class Layout:
    def __init__(self, nz, nx, nyl):
        self.nz, self.nx, self.nyl = nz, nx, nyl
        self.chips = nx * nyl
        last = nz // 2
        self.direct = (3, 1) if nz == 16 else (1,)
        self.relays = {1: (2,), 3: (6, 4), 6: (8, 7, 5)} if nz == 16 else {1: (2,)}
        distances = (1, 3, 2, 4, 6, 5, 7) if nz == 16 else (1,)
        arrivals = [0] + [d * s for d in distances for s in (1, -1)] + [nz // 2]
        order = [(d, yr) for yr in (0, 1) for d in arrivals]
        self.order = order

    def slot(self, dz, yr):
        dz = dz % self.nz
        return self.order.index((dz if dz <= self.nz // 2 else dz - self.nz, yr))


def kernel(lay, rows, w_hbm, a_hbm, ga_hbm, gb_hbm, wg_ref, ig_ref,
           w, g, ga, gat, gb, q, ysend, yrecv, tot, zsend, zrecv,
           p, csend, crecv, own, rsend, rrecv, d, acc,
           load_sem, ag_send, ag_recv, y_send, y_recv, z_send, z_recv,
           c_send, c_recv, r_send, r_recv, d_send, d_recv, f_send, f_recv):
    nz, nx, nyl = lay.nz, lay.nx, lay.nyl
    tensor, pipe = lax.axis_index("tensor"), lax.axis_index("pipe")
    z, yh = tensor // 2, tensor % 2
    core, chip = pipe % 2, pipe // 2
    yl, x = chip // nx, chip % nx
    half_rows = nz * rows
    core_rows = half_rows // 2

    def at_tensor(dz, dy):
        return {"tensor": ((z + dz + nz) % nz) * 2 + (yh + dy) % 2}

    def at_chip(dyl, dx):
        return {"pipe": (((yl + dyl) % nyl) * nx + (x + dx) % nx) * 2 + core}

    other_core = {"pipe": chip * 2 + (1 - core)}
    others = [(a, b) for a in range(nyl) for b in range(nx) if a or b]

    def remote(src, dst, send, recv, to):
        return pltpu.make_async_remote_copy(
            src_ref=src, dst_ref=dst, send_sem=send, recv_sem=recv, device_id=to, device_id_type=MESH)

    sent = []

    def block(slot):
        return g.at[pl.ds(slot * rows, rows)]

    load_a = pltpu.make_async_copy(a_hbm, block(lay.slot(0, 0)), load_sem.at[0])
    load_w = pltpu.make_async_copy(w_hbm, w, load_sem.at[1])
    load_gb = pltpu.make_async_copy(gb_hbm, gb, load_sem.at[2])
    load_a.start()
    load_w.start()
    load_gb.start()
    load_ga, ga_row = [], []
    lanes = ga.shape[2]
    for half in range(2):
        dz, yr = 0, 0
        for j in range(nz):
            hit = 1 - jnp.minimum(jnp.abs(core * lay.chips + chip - j), 1)
            block_z, block_y = lay.order[half * nz + j]
            dz, yr = dz + hit * (block_z % nz), yr + hit * block_y
        t = ((z + dz) % nz) * 2 + (yh + yr) % 2
        start = pl.multiple_of((t * rows // lanes) * lanes, lanes)
        c = pltpu.make_async_copy(ga_hbm.at[:, pl.ds(start, lanes)], ga.at[half], load_sem.at[3 + half])
        c.start()
        load_ga.append(c)
        ga_row.append(pl.multiple_of(t * rows % lanes, rows))

    barrier = pltpu.get_barrier_semaphore()
    greet = [at_tensor(dz, 0) for d in range(1, min(4, nz // 2)) for dz in (d, -d)] + [at_tensor(0, 1), other_core]
    greet += [at_chip(*o) for o in others]
    for to in greet:
        pl.semaphore_signal(barrier, inc=1, device_id=to, device_id_type=MESH)
    pl.semaphore_wait(barrier, len(greet))

    def gather(src, dz, yr, to):
        s = lay.slot(dz, yr)
        return remote(src, block(s), ag_send.at[s], ag_recv.at[s], to)

    def start_gather():
        copies = [gather(a_hbm, d * s, 0, at_tensor(-d * s, 0)) for d in lay.direct for s in (1, -1)]
        copies.insert(len(copies) - 2, gather(a_hbm, 0, 1, at_tensor(0, 1)))
        for c in copies:
            c.start()
        sent.extend(copies)

    def arrive(dz, yr):
        src = block(lay.slot(dz, yr))
        gather(src, dz, yr, at_tensor(1, 0)).wait_recv()
        if yr == 0:
            sign = 1 if dz > 0 else -1
            copies = []
            for d in lay.relays.get(abs(dz), ()):
                if d < nz // 2 or dz > 0:
                    copies.append(gather(src, d * sign, 0, at_tensor(dz - d * sign, 0)))
            copies.append(gather(src, dz, 1, at_tensor(0, 1)))
            for c in copies:
                c.start()
            sent.extend(copies)

    width = w.shape[1]
    yc = remote(ysend, yrecv, y_send, y_recv, at_tensor(0, 1))

    def local_b():
        load_gb.wait()
        load_w.wait()
        q[...] = lax.dot_general(gb[...], w[...], (((0,), (0,)), ((), ())), preferred_element_type=F32).reshape(q.shape)
        ysend[...] = q[:, pl.ds(1 - yh, 1)].reshape(nz * q.shape[2], width).astype(BF16)

    def exchange_b():
        yc.start()
        sent.append(yc)

    def turn_ga():
        for half in range(2):
            load_ga[half].wait()
            gat[half] = ga[half].T

    def sum_b():
        yc.wait_recv()
        tot[:, 0:width] = q[:, pl.ds(yh, 1)].reshape(nz * q.shape[2], width) + yrecv[...].astype(F32)
        wide = 2 * zsend.shape[2]
        if wide > width:
            tot[:, width:wide] = jnp.zeros((tot.shape[0], wide - width), F32)
        left = tot[:, 0:wide // 2].reshape(nz, q.shape[2], wide // 2)
        right = tot[:, wide // 2:wide].reshape(nz, q.shape[2], wide // 2)
        zsend[...] = jnp.concatenate([left, right], axis=1).astype(BF16)

    zcs = []

    def send_b():
        for dz in [s * k for k in range(1, nz // 2 + 1) for s in (1, -1)][:nz - 1]:
            c = remote(zsend.at[(z + dz + nz) % nz], zrecv.at[dz % nz], z_send.at[dz % nz], z_recv.at[dz % nz], at_tensor(dz, 0))
            c.start()
            zcs.append(c)

    def finish_b():
        depth = q.shape[2]
        wide = zsend.shape[2]
        mine = tot[pl.ds(pl.multiple_of(z * depth, depth), depth), :]
        total = jnp.concatenate([mine[:, 0:wide], mine[:, wide:2 * wide]], axis=0)
        for c in zcs:
            c.wait_recv()
        for dz in range(1, nz):
            total += zrecv[dz].astype(F32)
        ig_ref[:, 0:wide] = total[0:depth].astype(BF16)
        ig_ref[:, wide:width] = total[depth:2 * depth, 0:width - wide].astype(BF16)

    core_copies, chip_copies, delta_copies, core_forwards = [None, None], [[], []], [[], []], [[], []]

    def project(half):
        p[half] = lax.dot_general(
            g[pl.ds(half * half_rows, half_rows), :], w[...], (((1,), (1,)), ((), ())), preferred_element_type=F32)
        csend[half] = p[half, pl.ds(pl.multiple_of((1 - core) * core_rows, core_rows), core_rows), :].astype(BF16)
        c = remote(csend.at[half], crecv.at[half], c_send.at[half], c_recv.at[half], other_core)
        c.start()
        core_copies[half] = c

    def reduce_send(half):
        core_copies[half].wait_recv()
        own[half] = p[half, pl.ds(pl.multiple_of(core * core_rows, core_rows), core_rows), :] + crecv[half].astype(F32)
        rsend[half] = own[half].astype(BF16)
        for k, (dyl, dx) in enumerate(others):
            to = ((yl + dyl) % nyl) * nx + (x + dx) % nx
            c = remote(rsend.at[half, pl.ds(pl.multiple_of(to * rows, rows), rows)], rrecv.at[half, k],
                       r_send.at[half, k], r_recv.at[half, k], at_chip(dyl, dx))
            c.start()
            chip_copies[half].append(c)

    def d_block(half, which_core, which_chip):
        start = ((half * 2 + which_core) * lay.chips + which_chip) * rows
        return d.at[pl.ds(pl.multiple_of(start, rows), rows)]

    def activate(half):
        for c in chip_copies[half]:
            c.wait_recv()
        pre = own[half, pl.ds(pl.multiple_of(chip * rows, rows), rows), :]
        for k in range(len(others)):
            pre += rrecv[half, k].astype(F32)
        mine = d_block(half, core, chip)
        mine[...] = (gat[half, pl.ds(ga_row[half], rows), :].astype(F32) * slope(pre)).astype(BF16)
        for k, (dyl, dx) in enumerate(others):
            c = remote(mine, mine, d_send.at[half, k], d_recv.at[half, k], at_chip(dyl, dx))
            c.start()
            delta_copies[half].append(c)
        n = len(others)
        c = remote(mine, mine, f_send.at[half, n], f_recv.at[half, n], other_core)
        c.start()
        core_forwards[half].append(c)

    def spread(half):
        for k, (dyl, dx) in enumerate(others):
            source = ((yl - dyl + nyl) % nyl) * nx + (x - dx + nx) % nx
            b = d_block(half, core, source)
            remote(b, b, d_send.at[half, k], d_recv.at[half, k], at_chip(dyl, dx)).wait_recv()
            c = remote(b, b, f_send.at[half, k], f_recv.at[half, k], other_core)
            c.start()
            core_forwards[half].append(c)

    def collect(half):
        for k, (dyl, dx) in enumerate(others):
            source = ((yl - dyl + nyl) % nyl) * nx + (x - dx + nx) % nx
            b = d_block(half, 1 - core, source)
            remote(b, b, f_send.at[half, k], f_recv.at[half, k], other_core).wait_recv()
        n = len(others)
        b = d_block(half, 1 - core, chip)
        remote(b, b, f_send.at[half, n], f_recv.at[half, n], other_core).wait_recv()

    def weight(half, lo, hi):
        return lax.dot_general(
            d[pl.ds(half * half_rows, half_rows), lo:hi], g[pl.ds(half * half_rows, half_rows), :],
            (((0,), (0,)), ((), ())), preferred_element_type=F32)

    hid = w.shape[0]
    cuts = list(range(0, hid, 256)) + [hid]

    def weigh(half):
        if half == 0:
            for lo, hi in zip(cuts[:-1], cuts[1:]):
                acc[lo:hi, :] = weight(0, lo, hi)
            return
        for lo, hi in zip(cuts[:-1], cuts[1:]):
            wg_ref[lo:hi, :] = (acc[lo:hi, :] + weight(1, lo, hi)).astype(BF16)

    start_gather()
    local_b()
    exchange_b()
    for b in lay.order[1:nz]:
        arrive(*b)
    load_a.wait()
    project(0)
    turn_ga()
    reduce_send(0)
    for b in lay.order[nz:]:
        arrive(*b)
    project(1)
    sum_b()
    send_b()
    reduce_send(1)
    activate(0)
    activate(1)
    spread(0)
    finish_b()
    collect(0)
    weigh(0)
    spread(1)
    collect(1)
    weigh(1)
    for c in sent + zcs + core_copies + chip_copies[0] + chip_copies[1] + delta_copies[0] + delta_copies[1]:
        c.wait_send()
    for c in core_forwards[0] + core_forwards[1]:
        c.wait_send()


def build(mesh, lay):
    def step(w_up, inputs_a, grad_a, grad_b):
        hid, width = w_up.shape
        rows = inputs_a.shape[0]
        nz = lay.nz
        seq_b = grad_b.shape[0]
        depth = seq_b // (2 * nz)
        half_rows = nz * rows
        n = lay.chips - 1
        wide = -(-width // 256) * 128
        dma = pltpu.SemaphoreType.DMA
        flops = 2 * hid * width * (4 * half_rows + seq_b)
        return pl.pallas_call(
            functools.partial(kernel, lay, rows),
            out_shape=(jax.ShapeDtypeStruct((hid, width), BF16), jax.ShapeDtypeStruct((depth, width), BF16)),
            in_specs=[pl.BlockSpec(memory_space=pl.ANY)] * 4,
            out_specs=(pl.BlockSpec(memory_space=pltpu.VMEM), pl.BlockSpec(memory_space=pltpu.VMEM)),
            scratch_shapes=[
                pltpu.VMEM((hid, width), BF16),
                pltpu.VMEM((2 * half_rows, width), BF16),
                pltpu.VMEM((2, hid, 128), BF16),
                pltpu.VMEM((2, 128, hid), BF16),
                pltpu.VMEM((hid, seq_b), BF16),
                pltpu.VMEM((nz, 2, depth, width), F32),
                pltpu.VMEM((nz * depth, width), BF16),
                pltpu.VMEM((nz * depth, width), BF16),
                pltpu.VMEM((nz * depth, 2 * wide), F32),
                pltpu.VMEM((nz, 2 * depth, wide), BF16),
                pltpu.VMEM((nz, 2 * depth, wide), BF16),
                pltpu.VMEM((2, half_rows, hid), F32),
                pltpu.VMEM((2, half_rows // 2, hid), BF16),
                pltpu.VMEM((2, half_rows // 2, hid), BF16),
                pltpu.VMEM((2, half_rows // 2, hid), F32),
                pltpu.VMEM((2, half_rows // 2, hid), BF16),
                pltpu.VMEM((2, n, rows, hid), BF16),
                pltpu.VMEM((2 * half_rows, hid), BF16),
                pltpu.VMEM((hid, width), F32),
                dma((5,)), dma((2 * nz,)), dma((2 * nz,)), dma, dma, dma((nz,)), dma((nz,)),
                dma((2,)), dma((2,)), dma((2, n)), dma((2, n)), dma((2, n)), dma((2, n)), dma((2, n + 1)), dma((2, n + 1)),
            ],
            compiler_params=pltpu.CompilerParams(
                collective_id=0, has_side_effects=True, vmem_limit_bytes=36 * 1024 * 1024),
            cost_estimate=pl.CostEstimate(flops=flops, bytes_accessed=5_000_000, transcendentals=100_000),
        )(*[pltpu.with_memory_space_constraint(v, pltpu.HBM) for v in (w_up, inputs_a, grad_a.T, grad_b.T)])

    return jax.shard_map(
        step,
        mesh=mesh,
        in_specs=(P("tensor", "pipe"), P("tensor", "pipe"), P(None, "tensor"), P(None, "tensor")),
        out_specs=(P("tensor", "pipe"), P("tensor", "pipe")),
        check_vma=False,
    )


def solution(mesh):
    nz = mesh.shape["tensor"] // 2
    nyl = 2
    return build(mesh, Layout(nz, mesh.shape["pipe"] // (2 * nyl), nyl))
```

```python
import functools

import jax
import jax.numpy as jnp
from jax import lax
from jax.experimental import pallas as pl
from jax.experimental.pallas import tpu as pltpu
from jax.sharding import PartitionSpec as P

MESH = pl.DeviceIdType.MESH
F32 = jnp.float32
BF16 = jnp.bfloat16


def slope(pre):
    cdf = 0.5 * (1.0 + lax.erf(pre * 0.7071067811865476))
    pdf = jnp.exp(-0.5 * pre * pre) * 0.3989422804014327
    return cdf + pre * pdf


class Layout:
    def __init__(self, nz, nx, nyl):
        self.nz, self.nx, self.nyl = nz, nx, nyl
        self.chips = nx * nyl
        last = nz // 2
        self.direct = (3, 1) if nz == 16 else (1,)
        self.relays = {1: (2,), 3: (6, 4), 6: (8, 7, 5)} if nz == 16 else {1: (2,)}
        self.last_hop = (5, 7, 8) if nz == 16 else ()
        self.across = (6,) if nz == 16 else ()
        last = nz // 2
        pairs = lambda ds: [d * s for d in ds for s in (1, -1)]
        if nz == 16:
            own, other = pairs((1, 3, 2, 4, 6)), pairs((1, 3))
            own_far, other_far = pairs((5, 7)) + [last], pairs((2, 4, 6, 5, 7)) + [last]
        else:
            own, other, own_far, other_far = pairs((1,)), [], [last], pairs((1,)) + [last]
        self.relayed = [(d, 0) for d in own]
        order = [(d, 0) for d in [0] + own] + [(d, 1) for d in [0] + other]
        order = order + [(d, 0) for d in own_far] + [(d, 1) for d in other_far]
        self.order = order

    def slot(self, dz, yr):
        dz = dz % self.nz
        return self.order.index((dz if dz <= self.nz // 2 else dz - self.nz, yr))


def kernel(lay, rows, w_hbm, a_hbm, ga_hbm, gb_hbm, wg_ref, ig_ref,
           w, g, ga, gat, gb, q, ysend, yrecv, tot, zsend, zrecv,
           p, csend, crecv, own, rsend, rrecv, d, acc,
           load_sem, ag_send, ag_recv, y_send, y_recv, z_send, z_recv,
           c_send, c_recv, r_send, r_recv, d_send, d_recv, f_send, f_recv):
    nz, nx, nyl = lay.nz, lay.nx, lay.nyl
    tensor, pipe = lax.axis_index("tensor"), lax.axis_index("pipe")
    z, yh = tensor // 2, tensor % 2
    core, chip = pipe % 2, pipe // 2
    yl, x = chip // nx, chip % nx
    half_rows = nz * rows
    core_rows = half_rows // 2

    def at_tensor(dz, dy):
        return {"tensor": ((z + dz + nz) % nz) * 2 + (yh + dy) % 2}

    def at_chip(dyl, dx):
        return {"pipe": (((yl + dyl) % nyl) * nx + (x + dx) % nx) * 2 + core}

    other_core = {"pipe": chip * 2 + (1 - core)}
    others = [(a, b) for a in range(nyl) for b in range(nx) if a or b]

    def remote(src, dst, send, recv, to):
        return pltpu.make_async_remote_copy(
            src_ref=src, dst_ref=dst, send_sem=send, recv_sem=recv, device_id=to, device_id_type=MESH)

    sent = []

    def block(slot):
        return g.at[pl.ds(slot * rows, rows)]

    barrier = pltpu.get_barrier_semaphore()
    greet = [at_tensor(d * s, 0) for d in lay.direct for s in (1, -1)] + [at_tensor(0, 1), other_core]
    greet += [at_chip(*o) for o in others]
    for to in greet:
        pl.semaphore_signal(barrier, inc=1, device_id=to, device_id_type=MESH)

    load_a = pltpu.make_async_copy(a_hbm, block(lay.slot(0, 0)), load_sem.at[0])
    load_w = pltpu.make_async_copy(w_hbm, w, load_sem.at[1])
    load_gb = pltpu.make_async_copy(gb_hbm, gb, load_sem.at[2])
    load_a.start()
    load_w.start()
    load_gb.start()
    pl.semaphore_wait(barrier, len(greet))

    def gather(src, dz, yr, to):
        s = lay.slot(dz, yr)
        return remote(src, block(s), ag_send.at[s], ag_recv.at[s], to)

    def start_gather():
        copies = [gather(a_hbm, d * s, 0, at_tensor(-d * s, 0)) for d in lay.direct for s in (1, -1)]
        copies.insert(len(copies) - 2, gather(a_hbm, 0, 1, at_tensor(0, 1)))
        for c in copies:
            c.start()
        sent.extend(copies)

    def arrive(dz, yr):
        src = block(lay.slot(dz, yr))
        gather(src, dz, yr, at_tensor(1, 0)).wait_recv()
        if yr == 0:
            sign = 1 if dz > 0 else -1
            copies = []
            reached = abs(dz)
            for d in lay.relays.get(reached, ()):
                if d < nz // 2 or dz > 0:
                    for dy in (0, 1) if reached in lay.across else (0,):
                        copies.append(gather(src, d * sign, dy, at_tensor(dz - d * sign, dy)))
            if reached not in lay.last_hop:
                copies.append(gather(src, dz, 1, at_tensor(0, 1)))
            for c in copies:
                c.start()
            sent.extend(copies)

    width = w.shape[1]
    yc = remote(ysend, yrecv, y_send, y_recv, at_tensor(0, 1))

    def local_b():
        load_gb.wait()
        load_w.wait()
        q[...] = lax.dot_general(gb[...], w[...], (((0,), (0,)), ((), ())), preferred_element_type=F32).reshape(q.shape)
        ysend[...] = q[:, pl.ds(1 - yh, 1)].reshape(nz * q.shape[2], width).astype(BF16)

    def exchange_b():
        yc.start()
        sent.append(yc)

    load_ga, ga_row = [], []
    lanes = ga.shape[2]

    def start_ga():
        for half in range(2):
            dz, yr = 0, 0
            for j in range(nz):
                hit = 1 - jnp.minimum(jnp.abs(core * lay.chips + chip - j), 1)
                block_z, block_y = lay.order[half * nz + j]
                dz, yr = dz + hit * (block_z % nz), yr + hit * block_y
            t = ((z + dz) % nz) * 2 + (yh + yr) % 2
            start = pl.multiple_of((t * rows // lanes) * lanes, lanes)
            c = pltpu.make_async_copy(ga_hbm.at[:, pl.ds(start, lanes)], ga.at[half], load_sem.at[3 + half])
            c.start()
            load_ga.append(c)
            ga_row.append(pl.multiple_of(t * rows % lanes, rows))

    def turn_ga():
        for half in range(2):
            load_ga[half].wait()
            gat[half] = ga[half].T

    def sum_b():
        yc.wait_recv()
        tot[:, 0:width] = q[:, pl.ds(yh, 1)].reshape(nz * q.shape[2], width) + yrecv[...].astype(F32)
        wide = 2 * zsend.shape[2]
        if wide > width:
            tot[:, width:wide] = jnp.zeros((tot.shape[0], wide - width), F32)
        left = tot[:, 0:wide // 2].reshape(nz, q.shape[2], wide // 2)
        right = tot[:, wide // 2:wide].reshape(nz, q.shape[2], wide // 2)
        zsend[...] = jnp.concatenate([left, right], axis=1).astype(BF16)

    zcs = []

    def send_b(blocks):
        for dz in [block_z for block_z, block_y in blocks if block_z and block_y == 0]:
            c = remote(zsend.at[(z + dz + nz) % nz], zrecv.at[dz % nz], z_send.at[dz % nz], z_recv.at[dz % nz], at_tensor(dz, 0))
            c.start()
            zcs.append(c)

    def finish_b():
        depth = q.shape[2]
        wide = zsend.shape[2]
        mine = tot[pl.ds(pl.multiple_of(z * depth, depth), depth), :]
        total = jnp.concatenate([mine[:, 0:wide], mine[:, wide:2 * wide]], axis=0)
        for c in zcs:
            c.wait_recv()
        for dz in range(1, nz):
            total += zrecv[dz].astype(F32)
        ig_ref[:, 0:wide] = total[0:depth].astype(BF16)
        ig_ref[:, wide:width] = total[depth:2 * depth, 0:width - wide].astype(BF16)

    core_copies, chip_copies, delta_copies, core_forwards = [None, None], [[], []], [[], []], [[], []]

    def project(half):
        p[half] = lax.dot_general(
            g[pl.ds(half * half_rows, half_rows), :], w[...], (((1,), (1,)), ((), ())), preferred_element_type=F32)
        csend[half] = p[half, pl.ds(pl.multiple_of((1 - core) * core_rows, core_rows), core_rows), :].astype(BF16)
        c = remote(csend.at[half], crecv.at[half], c_send.at[half], c_recv.at[half], other_core)
        c.start()
        core_copies[half] = c

    def reduce_send(half):
        core_copies[half].wait_recv()
        own[half] = p[half, pl.ds(pl.multiple_of(core * core_rows, core_rows), core_rows), :] + crecv[half].astype(F32)
        rsend[half] = own[half].astype(BF16)
        for k, (dyl, dx) in enumerate(others):
            to = ((yl + dyl) % nyl) * nx + (x + dx) % nx
            c = remote(rsend.at[half, pl.ds(pl.multiple_of(to * rows, rows), rows)], rrecv.at[half, k],
                       r_send.at[half, k], r_recv.at[half, k], at_chip(dyl, dx))
            c.start()
            chip_copies[half].append(c)

    def d_block(half, which_core, which_chip):
        start = ((half * 2 + which_core) * lay.chips + which_chip) * rows
        return d.at[pl.ds(pl.multiple_of(start, rows), rows)]

    def activate(half):
        for c in chip_copies[half]:
            c.wait_recv()
        pre = own[half, pl.ds(pl.multiple_of(chip * rows, rows), rows), :]
        for k in range(len(others)):
            pre += rrecv[half, k].astype(F32)
        mine = d_block(half, core, chip)
        mine[...] = (gat[half, pl.ds(ga_row[half], rows), :].astype(F32) * slope(pre)).astype(BF16)
        for k, (dyl, dx) in enumerate(others):
            c = remote(mine, mine, d_send.at[half, k], d_recv.at[half, k], at_chip(dyl, dx))
            c.start()
            delta_copies[half].append(c)
        n = len(others)
        c = remote(mine, mine, f_send.at[half, n], f_recv.at[half, n], other_core)
        c.start()
        core_forwards[half].append(c)

    def spread(half):
        for k, (dyl, dx) in enumerate(others):
            source = ((yl - dyl + nyl) % nyl) * nx + (x - dx + nx) % nx
            b = d_block(half, core, source)
            remote(b, b, d_send.at[half, k], d_recv.at[half, k], at_chip(dyl, dx)).wait_recv()
            c = remote(b, b, f_send.at[half, k], f_recv.at[half, k], other_core)
            c.start()
            core_forwards[half].append(c)

    def collect(half):
        for k, (dyl, dx) in enumerate(others):
            source = ((yl - dyl + nyl) % nyl) * nx + (x - dx + nx) % nx
            b = d_block(half, 1 - core, source)
            remote(b, b, f_send.at[half, k], f_recv.at[half, k], other_core).wait_recv()
        n = len(others)
        b = d_block(half, 1 - core, chip)
        remote(b, b, f_send.at[half, n], f_recv.at[half, n], other_core).wait_recv()

    def weight(half, lo, hi):
        return lax.dot_general(
            d[pl.ds(half * half_rows, half_rows), lo:hi], g[pl.ds(half * half_rows, half_rows), :],
            (((0,), (0,)), ((), ())), preferred_element_type=F32)

    hid = w.shape[0]
    cuts = list(range(0, hid, 256)) + [hid]

    def weigh(half):
        if half == 0:
            for lo, hi in zip(cuts[:-1], cuts[1:]):
                acc[lo:hi, :] = weight(0, lo, hi)
            return
        for lo, hi in zip(cuts[:-1], cuts[1:]):
            wg_ref[lo:hi, :] = (acc[lo:hi, :] + weight(1, lo, hi)).astype(BF16)

    start_gather()
    local_b()
    exchange_b()
    start_ga()
    for b in lay.relayed:
        arrive(*b)
    for b in lay.order[1:nz]:
        if b not in lay.relayed:
            arrive(*b)
    load_a.wait()
    project(0)
    turn_ga()
    sum_b()
    reduce_send(0)
    send_b(lay.order[:nz])
    for b in lay.order[nz:]:
        arrive(*b)
    send_b(lay.order[nz:])
    project(1)
    reduce_send(1)
    activate(0)
    activate(1)
    spread(0)
    collect(0)
    weigh(0)
    spread(1)
    collect(1)
    finish_b()
    weigh(1)
    for c in sent + zcs + core_copies + chip_copies[0] + chip_copies[1] + delta_copies[0] + delta_copies[1]:
        c.wait_send()
    for c in core_forwards[0] + core_forwards[1]:
        c.wait_send()


def build(mesh, lay):
    def step(w_up, inputs_a, grad_a, grad_b):
        hid, width = w_up.shape
        rows = inputs_a.shape[0]
        nz = lay.nz
        seq_b = grad_b.shape[0]
        depth = seq_b // (2 * nz)
        half_rows = nz * rows
        n = lay.chips - 1
        wide = -(-width // 256) * 128
        dma = pltpu.SemaphoreType.DMA
        flops = 2 * hid * width * (4 * half_rows + seq_b)
        return pl.pallas_call(
            functools.partial(kernel, lay, rows),
            out_shape=(jax.ShapeDtypeStruct((hid, width), BF16), jax.ShapeDtypeStruct((depth, width), BF16)),
            in_specs=[pl.BlockSpec(memory_space=pl.ANY)] * 4,
            out_specs=(pl.BlockSpec(memory_space=pltpu.VMEM), pl.BlockSpec(memory_space=pltpu.VMEM)),
            scratch_shapes=[
                pltpu.VMEM((hid, width), BF16),
                pltpu.VMEM((2 * half_rows, width), BF16),
                pltpu.VMEM((2, hid, 128), BF16),
                pltpu.VMEM((2, 128, hid), BF16),
                pltpu.VMEM((hid, seq_b), BF16),
                pltpu.VMEM((nz, 2, depth, width), F32),
                pltpu.VMEM((nz * depth, width), BF16),
                pltpu.VMEM((nz * depth, width), BF16),
                pltpu.VMEM((nz * depth, 2 * wide), F32),
                pltpu.VMEM((nz, 2 * depth, wide), BF16),
                pltpu.VMEM((nz, 2 * depth, wide), BF16),
                pltpu.VMEM((2, half_rows, hid), F32),
                pltpu.VMEM((2, half_rows // 2, hid), BF16),
                pltpu.VMEM((2, half_rows // 2, hid), BF16),
                pltpu.VMEM((2, half_rows // 2, hid), F32),
                pltpu.VMEM((2, half_rows // 2, hid), BF16),
                pltpu.VMEM((2, n, rows, hid), BF16),
                pltpu.VMEM((2 * half_rows, hid), BF16),
                pltpu.VMEM((hid, width), F32),
                dma((5,)), dma((2 * nz,)), dma((2 * nz,)), dma, dma, dma((nz,)), dma((nz,)),
                dma((2,)), dma((2,)), dma((2, n)), dma((2, n)), dma((2, n)), dma((2, n)), dma((2, n + 1)), dma((2, n + 1)),
            ],
            compiler_params=pltpu.CompilerParams(
                collective_id=0, has_side_effects=True, vmem_limit_bytes=36 * 1024 * 1024),
            cost_estimate=pl.CostEstimate(flops=flops, bytes_accessed=5_000_000, transcendentals=100_000),
        )(*[pltpu.with_memory_space_constraint(v, pltpu.HBM) for v in (w_up, inputs_a, grad_a.T, grad_b.T)])

    return jax.shard_map(
        step,
        mesh=mesh,
        in_specs=(P("tensor", "pipe"), P("tensor", "pipe"), P(None, "tensor"), P(None, "tensor")),
        out_specs=(P("tensor", "pipe"), P("tensor", "pipe")),
        check_vma=False,
    )


def solution(mesh):
    nz = mesh.shape["tensor"] // 2
    nyl = 2
    return build(mesh, Layout(nz, mesh.shape["pipe"] // (2 * nyl), nyl))
```

```python
import functools

import jax
import jax.numpy as jnp
from jax import lax
from jax.experimental import pallas as pl
from jax.experimental.pallas import tpu as pltpu
from jax.sharding import PartitionSpec as P

MESH = pl.DeviceIdType.MESH
F32 = jnp.float32
BF16 = jnp.bfloat16


def slope(pre):
    cdf = 0.5 * (1.0 + lax.erf(pre * 0.7071067811865476))
    pdf = jnp.exp(-0.5 * pre * pre) * 0.3989422804014327
    return cdf + pre * pdf


class Layout:
    def __init__(self, nz, nx, nyl):
        self.nz, self.nx, self.nyl = nz, nx, nyl
        self.chips = nx * nyl
        last = nz // 2
        self.direct = (3, 1) if nz == 16 else (1,)
        self.relays = {1: (2,), 3: (6, 4), 4: (5,), 6: (8, 7)} if nz == 16 else {1: (2,)}
        self.last_hop = (5, 7, 8) if nz == 16 else ()
        self.across = (4, 6) if nz == 16 else ()
        last = nz // 2
        pairs = lambda ds: [d * s for d in ds for s in (1, -1)]
        if nz == 16:
            own, other = pairs((3, 1, 4, 2, 6)), pairs((1, 3))
            own_far, other_far = pairs((5, 7)) + [last], pairs((2, 4, 6, 5, 7)) + [last]
        else:
            own, other, own_far, other_far = pairs((1,)), [], [last], pairs((1,)) + [last]
        self.relayed = [(d, 0) for d in own]
        order = [(d, 0) for d in [0] + own] + [(d, 1) for d in [0] + other]
        order = order + [(d, 0) for d in own_far] + [(d, 1) for d in other_far]
        self.order = order

    def slot(self, dz, yr):
        dz = dz % self.nz
        return self.order.index((dz if dz <= self.nz // 2 else dz - self.nz, yr))


def kernel(lay, rows, w_hbm, a_hbm, ga_hbm, gb_hbm, acc, d_out, g_out, ig_ref,
           w, g, ga, gat, gb, q, ysend, yrecv, tot, zsend, zrecv,
           p, csend, crecv, own, rsend, rrecv, d,
           load_sem, ag_send, ag_recv, y_send, y_recv, z_send, z_recv,
           c_send, c_recv, r_send, r_recv, d_send, d_recv, f_send, f_recv):
    nz, nx, nyl = lay.nz, lay.nx, lay.nyl
    tensor, pipe = lax.axis_index("tensor"), lax.axis_index("pipe")
    z, yh = tensor // 2, tensor % 2
    core, chip = pipe % 2, pipe // 2
    yl, x = chip // nx, chip % nx
    half_rows = nz * rows
    core_rows = half_rows // 2

    def at_tensor(dz, dy):
        return {"tensor": ((z + dz + nz) % nz) * 2 + (yh + dy) % 2}

    def at_chip(dyl, dx):
        return {"pipe": (((yl + dyl) % nyl) * nx + (x + dx) % nx) * 2 + core}

    other_core = {"pipe": chip * 2 + (1 - core)}
    others = [(a, b) for a in range(nyl) for b in range(nx) if a or b]
    others.sort(key=lambda o: -(o[0] + min(o[1], nx - o[1])))

    def remote(src, dst, send, recv, to):
        return pltpu.make_async_remote_copy(
            src_ref=src, dst_ref=dst, send_sem=send, recv_sem=recv, device_id=to, device_id_type=MESH)

    sent = []

    def block(slot):
        return g.at[pl.ds(slot * rows, rows)]

    barrier = pltpu.get_barrier_semaphore()
    greet = [at_tensor(d * s, 0) for d in lay.direct for s in (1, -1)] + [at_tensor(0, 1), other_core]
    greet += [at_chip(*o) for o in others]
    for to in greet:
        pl.semaphore_signal(barrier, inc=1, device_id=to, device_id_type=MESH)

    load_a = pltpu.make_async_copy(a_hbm, block(lay.slot(0, 0)), load_sem.at[0])
    load_w = pltpu.make_async_copy(w_hbm, w, load_sem.at[1])
    load_gb = pltpu.make_async_copy(gb_hbm, gb, load_sem.at[2])
    load_a.start()
    load_w.start()
    load_gb.start()
    pl.semaphore_wait(barrier, len(greet))

    def gather(src, dz, yr, to):
        s = lay.slot(dz, yr)
        return remote(src, block(s), ag_send.at[s], ag_recv.at[s], to)

    def start_gather():
        copies = [gather(a_hbm, d * s, 0, at_tensor(-d * s, 0)) for d in lay.direct for s in (1, -1)]
        copies.insert(len(copies) - 2, gather(a_hbm, 0, 1, at_tensor(0, 1)))
        for c in copies:
            c.start()
        sent.extend(copies)

    def arrive(dz, yr):
        src = block(lay.slot(dz, yr))
        gather(src, dz, yr, at_tensor(1, 0)).wait_recv()
        if yr == 0:
            sign = 1 if dz > 0 else -1
            copies = []
            reached = abs(dz)
            for d in lay.relays.get(reached, ()):
                for dy in (0, 1) if reached in lay.across else (0,):
                    if d < nz // 2 or (dz > 0) == (dy == 0) or reached not in lay.across:
                        if d < nz // 2 or dz > 0 or reached in lay.across:
                            copies.append(gather(src, d * sign, dy, at_tensor(dz - d * sign, dy)))
            if reached not in lay.last_hop:
                copies.append(gather(src, dz, 1, at_tensor(0, 1)))
            for c in copies:
                c.start()
            sent.extend(copies)

    width = w.shape[1]
    yc = remote(ysend, yrecv, y_send, y_recv, at_tensor(0, 1))

    def local_b():
        load_gb.wait()
        load_w.wait()
        q[...] = lax.dot_general(gb[...], w[...], (((0,), (0,)), ((), ())), preferred_element_type=F32).reshape(q.shape)
        ysend[...] = q[:, pl.ds(1 - yh, 1)].reshape(nz * q.shape[2], width).astype(BF16)

    def exchange_b():
        yc.start()
        sent.append(yc)

    load_ga, ga_row = [], []
    lanes = ga.shape[2]

    def start_ga():
        for half in range(2):
            dz, yr = 0, 0
            for j in range(nz):
                hit = 1 - jnp.minimum(jnp.abs(core * lay.chips + chip - j), 1)
                block_z, block_y = lay.order[half * nz + j]
                dz, yr = dz + hit * (block_z % nz), yr + hit * block_y
            t = ((z + dz) % nz) * 2 + (yh + yr) % 2
            start = pl.multiple_of((t * rows // lanes) * lanes, lanes)
            c = pltpu.make_async_copy(ga_hbm.at[:, pl.ds(start, lanes)], ga.at[half], load_sem.at[3 + half])
            c.start()
            load_ga.append(c)
            ga_row.append(pl.multiple_of(t * rows % lanes, rows))

    def turn_ga():
        for half in range(2):
            load_ga[half].wait()
            gat[half] = ga[half].T

    def sum_b():
        yc.wait_recv()
        tot[:, 0:width] = q[:, pl.ds(yh, 1)].reshape(nz * q.shape[2], width) + yrecv[...].astype(F32)
        wide = 2 * zsend.shape[2]
        if wide > width:
            tot[:, width:wide] = jnp.zeros((tot.shape[0], wide - width), F32)
        left = tot[:, 0:wide // 2].reshape(nz, q.shape[2], wide // 2)
        right = tot[:, wide // 2:wide].reshape(nz, q.shape[2], wide // 2)
        zsend[...] = jnp.concatenate([left, right], axis=1).astype(BF16)

    zcs = []

    def send_b(blocks):
        for dz in sorted([block_z for block_z, block_y in blocks if block_z and block_y == 0], key=lambda block_z: -abs(block_z)):
            c = remote(zsend.at[(z + dz + nz) % nz], zrecv.at[dz % nz], z_send.at[dz % nz], z_recv.at[dz % nz], at_tensor(dz, 0))
            c.start()
            zcs.append(c)

    def finish_b():
        depth = q.shape[2]
        wide = zsend.shape[2]
        mine = tot[pl.ds(pl.multiple_of(z * depth, depth), depth), :]
        total = jnp.concatenate([mine[:, 0:wide], mine[:, wide:2 * wide]], axis=0)
        for c in zcs:
            c.wait_recv()
        for dz in range(1, nz):
            total += zrecv[dz].astype(F32)
        ig_ref[:, 0:wide] = total[0:depth].astype(BF16)
        ig_ref[:, wide:width] = total[depth:2 * depth, 0:width - wide].astype(BF16)

    core_copies, chip_copies, delta_copies, core_forwards = [None, None], [[], []], [[], []], [[], []]

    def project(half):
        p[half] = lax.dot_general(
            g[pl.ds(half * half_rows, half_rows), :], w[...], (((1,), (1,)), ((), ())), preferred_element_type=F32)
        csend[half] = p[half, pl.ds(pl.multiple_of((1 - core) * core_rows, core_rows), core_rows), :].astype(BF16)
        c = remote(csend.at[half], crecv.at[half], c_send.at[half], c_recv.at[half], other_core)
        c.start()
        core_copies[half] = c

    def reduce_send(half):
        core_copies[half].wait_recv()
        own[half] = p[half, pl.ds(pl.multiple_of(core * core_rows, core_rows), core_rows), :] + crecv[half].astype(F32)
        rsend[half] = own[half].astype(BF16)
        for k, (dyl, dx) in enumerate(others):
            to = ((yl + dyl) % nyl) * nx + (x + dx) % nx
            c = remote(rsend.at[half, pl.ds(pl.multiple_of(to * rows, rows), rows)], rrecv.at[half, k],
                       r_send.at[half, k], r_recv.at[half, k], at_chip(dyl, dx))
            c.start()
            chip_copies[half].append(c)

    def d_block(half, which_core, which_chip):
        start = ((half * 2 + which_core) * lay.chips + which_chip) * rows
        return d.at[pl.ds(pl.multiple_of(start, rows), rows)]

    def activate(half):
        for c in chip_copies[half]:
            c.wait_recv()
        pre = own[half, pl.ds(pl.multiple_of(chip * rows, rows), rows), :]
        for k in range(len(others)):
            pre += rrecv[half, k].astype(F32)
        mine = d_block(half, core, chip)
        mine[...] = (gat[half, pl.ds(ga_row[half], rows), :].astype(F32) * slope(pre)).astype(BF16)
        for k, (dyl, dx) in enumerate(others):
            c = remote(mine, mine, d_send.at[half, k], d_recv.at[half, k], at_chip(dyl, dx))
            c.start()
            delta_copies[half].append(c)
        n = len(others)
        c = remote(mine, mine, f_send.at[half, n], f_recv.at[half, n], other_core)
        c.start()
        core_forwards[half].append(c)

    def spread(half):
        for k, (dyl, dx) in reversed(list(enumerate(others))):
            source = ((yl - dyl + nyl) % nyl) * nx + (x - dx + nx) % nx
            b = d_block(half, core, source)
            remote(b, b, d_send.at[half, k], d_recv.at[half, k], at_chip(dyl, dx)).wait_recv()
            c = remote(b, b, f_send.at[half, k], f_recv.at[half, k], other_core)
            c.start()
            core_forwards[half].append(c)

    def collect(half):
        for k, (dyl, dx) in enumerate(others):
            source = ((yl - dyl + nyl) % nyl) * nx + (x - dx + nx) % nx
            b = d_block(half, 1 - core, source)
            remote(b, b, f_send.at[half, k], f_recv.at[half, k], other_core).wait_recv()
        n = len(others)
        b = d_block(half, 1 - core, chip)
        remote(b, b, f_send.at[half, n], f_recv.at[half, n], other_core).wait_recv()

    def weight(half, lo, hi):
        return lax.dot_general(
            d[pl.ds(half * half_rows, half_rows), lo:hi], g[pl.ds(half * half_rows, half_rows), :],
            (((0,), (0,)), ((), ())), preferred_element_type=F32)

    hid = w.shape[0]
    cuts = list(range(0, hid, 256)) + [hid]

    def weigh():
        for lo, hi in zip(cuts[:-1], cuts[1:]):
            acc[lo:hi, :] = weight(0, lo, hi)

    start_gather()
    local_b()
    exchange_b()
    start_ga()
    for b in lay.relayed:
        arrive(*b)
    for b in lay.order[1:nz]:
        if b not in lay.relayed:
            arrive(*b)
    load_a.wait()
    project(0)
    turn_ga()
    sum_b()
    send_b(lay.order[:nz])
    reduce_send(0)
    for b in lay.order[nz:]:
        arrive(*b)
    send_b(lay.order[nz:])
    project(1)
    reduce_send(1)
    g_out[...] = g[half_rows:2 * half_rows, :]
    activate(0)
    activate(1)
    spread(0)
    collect(0)
    weigh()
    spread(1)
    collect(1)
    finish_b()
    d_out[...] = d[half_rows:2 * half_rows, :]
    for c in sent + zcs + core_copies + chip_copies[0] + chip_copies[1] + delta_copies[0] + delta_copies[1]:
        c.wait_send()
    for c in core_forwards[0] + core_forwards[1]:
        c.wait_send()


def finish_kernel(acc, d, g, ig, wg_hbm, ig_hbm, out, sem):
    copies = [pltpu.make_async_copy(ig, ig_hbm, sem.at[0])]
    copies[0].start()
    hid = out.shape[0]
    cuts = list(range(0, hid, 256)) + [hid]
    for i, (lo, hi) in enumerate(zip(cuts[:-1], cuts[1:])):
        product = lax.dot_general(d[:, lo:hi], g[...], (((0,), (0,)), ((), ())), preferred_element_type=F32)
        out[lo:hi, :] = (acc[lo:hi, :] + product).astype(BF16)
        c = pltpu.make_async_copy(out.at[pl.ds(lo, hi - lo)], wg_hbm.at[pl.ds(lo, hi - lo)], sem.at[1 + i])
        c.start()
        copies.append(c)
    for c in copies:
        c.wait()


def build(mesh, lay):
    def step(w_up, inputs_a, grad_a, grad_b):
        hid, width = w_up.shape
        rows = inputs_a.shape[0]
        nz = lay.nz
        seq_b = grad_b.shape[0]
        depth = seq_b // (2 * nz)
        half_rows = nz * rows
        n = lay.chips - 1
        wide = -(-width // 256) * 128
        dma = pltpu.SemaphoreType.DMA
        flops = 2 * hid * width * (4 * half_rows + seq_b)
        parts = pl.pallas_call(
            functools.partial(kernel, lay, rows),
            out_shape=(jax.ShapeDtypeStruct((hid, width), F32), jax.ShapeDtypeStruct((half_rows, hid), BF16),
                       jax.ShapeDtypeStruct((half_rows, width), BF16), jax.ShapeDtypeStruct((depth, width), BF16)),
            in_specs=[pl.BlockSpec(memory_space=pl.ANY)] * 4,
            out_specs=(pl.BlockSpec(memory_space=pltpu.VMEM),) * 4,
            scratch_shapes=[
                pltpu.VMEM((hid, width), BF16),
                pltpu.VMEM((2 * half_rows, width), BF16),
                pltpu.VMEM((2, hid, 128), BF16),
                pltpu.VMEM((2, 128, hid), BF16),
                pltpu.VMEM((hid, seq_b), BF16),
                pltpu.VMEM((nz, 2, depth, width), F32),
                pltpu.VMEM((nz * depth, width), BF16),
                pltpu.VMEM((nz * depth, width), BF16),
                pltpu.VMEM((nz * depth, 2 * wide), F32),
                pltpu.VMEM((nz, 2 * depth, wide), BF16),
                pltpu.VMEM((nz, 2 * depth, wide), BF16),
                pltpu.VMEM((2, half_rows, hid), F32),
                pltpu.VMEM((2, half_rows // 2, hid), BF16),
                pltpu.VMEM((2, half_rows // 2, hid), BF16),
                pltpu.VMEM((2, half_rows // 2, hid), F32),
                pltpu.VMEM((2, half_rows // 2, hid), BF16),
                pltpu.VMEM((2, n, rows, hid), BF16),
                pltpu.VMEM((2 * half_rows, hid), BF16),
                dma((5,)), dma((2 * nz,)), dma((2 * nz,)), dma, dma, dma((nz,)), dma((nz,)),
                dma((2,)), dma((2,)), dma((2, n)), dma((2, n)), dma((2, n)), dma((2, n)), dma((2, n + 1)), dma((2, n + 1)),
            ],
            compiler_params=pltpu.CompilerParams(
                collective_id=0, has_side_effects=True, vmem_limit_bytes=36 * 1024 * 1024),
            cost_estimate=pl.CostEstimate(flops=flops, bytes_accessed=5_000_000, transcendentals=100_000),
        )(*[pltpu.with_memory_space_constraint(v, pltpu.HBM) for v in (w_up, inputs_a, grad_a.T, grad_b.T)])
        return pl.pallas_call(
            finish_kernel,
            out_shape=(jax.ShapeDtypeStruct((hid, width), BF16), jax.ShapeDtypeStruct((depth, width), BF16)),
            in_specs=[pl.BlockSpec(memory_space=pltpu.VMEM)] * 4,
            out_specs=(pl.BlockSpec(memory_space=pltpu.HBM),) * 2,
            scratch_shapes=[pltpu.VMEM((hid, width), BF16), dma((8,))],
            compiler_params=pltpu.CompilerParams(vmem_limit_bytes=16 * 1024 * 1024),
        )(*parts)

    return jax.shard_map(
        step,
        mesh=mesh,
        in_specs=(P("tensor", "pipe"), P("tensor", "pipe"), P(None, "tensor"), P(None, "tensor")),
        out_specs=(P("tensor", "pipe"), P("tensor", "pipe")),
        check_vma=False,
    )


def solution(mesh):
    nz = mesh.shape["tensor"] // 2
    nyl = 2
    return build(mesh, Layout(nz, mesh.shape["pipe"] // (2 * nyl), nyl))
```
